32 devices in a mesh: row: 4 (over z), col: 8 (over y, x, core).
Axes of the slice: x: 2, y: 2, z: 4, core: 2. Of those that a mesh axis runs over, the one named last changes fastest.
Arguments:
- pair: bfloat16 [192, 192, 128], P('row', 'col'), may hold values from -6 to 6
- chain_tokens: int32 [8], replicated, may hold values from 6 to 24, as said below
- w_in: bfloat16 [128, 640], replicated, may hold values from -0.5 to 0.5
- w_out: bfloat16 [128, 128], replicated, may hold values from -0.5 to 0.5
- grad_update: bfloat16 [192, 192, 128], P('row', 'col'), may hold values from -6 to 6
Outputs:
- update: bfloat16 [192, 192, 128], P('row', 'col')
- grad_pair: bfloat16 [192, 192, 128], P('row', 'col')
The draws below stay inside these ranges and needn't reach their ends.
Inputs may be any that keep to these rules, and one draw needn't show every extreme that they name: `chain_tokens`: one chain has exactly 24 real tokens and one has the fewest allowed.
All inputs are finite; a program needn't handle non-finite values.
Results may differ from the reference program's by a relative error of at most 0.014.
Values may be sent and summed in bfloat16 or wider, within the bound.
A program may use at most 256 MiB of HBM per device.

```python
import jax
import jax.numpy as jnp
from jax import lax

C = 128
CHAINS = 8
N = 192
N_ROW = 4
N_COL = 8


def draw_chain_tokens(key, part):
    key = jax.random.fold_in(key, 11)
    slot = N // CHAINS
    lowest = max(slot // 4, 1)
    first, second = jax.random.split(key, 2)
    counts = jax.random.randint(first, (CHAINS,), lowest, slot + 1, dtype=jnp.int32)
    order = jax.random.permutation(second, CHAINS)
    counts = counts.at[order[0]].set(slot)
    counts = counts.at[order[1]].set(lowest)
    return counts


def block_levels(stream_key, shape, cuts, least, top_value):
    factor_of = 1.0
    for position, blocks in cuts:
        draws = jax.random.uniform(jax.random.fold_in(jax.random.fold_in(stream_key, 6), position), (blocks,), jnp.float32, least / len(cuts), top_value / len(cuts))
        factor_of = factor_of * jnp.repeat(jnp.exp(draws), shape[position] // blocks).reshape((-1,) + (1,) * (len(shape) - 1 - position))
    return factor_of


def gaussian(own_key, shape, scale, limit, shards=(), kind=jnp.bfloat16):
    array = jax.random.normal(own_key, shape, jnp.float32) * scale
    if len(shards) > 0:
        array = block_levels(own_key, shape, shards, -0.22, 0.18) * array
    return jnp.clip(array, min=-limit, max=limit).astype(kind)


def setup_inputs(seed: int = 0) -> dict:
    key_of = jax.random.split(jax.random.key(seed), 6)
    pair = gaussian(key_of[0], (N, N, C), 1.0, 6.0, ((0, 4), (1, 8)))
    chain_tokens = draw_chain_tokens(jax.random.fold_in(key_of[5], 71), 0)
    w_in = gaussian(key_of[2], (C, 5 * C), C ** -0.5, 0.5)
    w_out = gaussian(key_of[3], (C, C), C ** -0.5, 0.5)
    grad_update = gaussian(key_of[4], (N, N, C), 1.0, 6.0, ((0, 4), (1, 8)))
    return {"pair": pair, "chain_tokens": chain_tokens, "w_in": w_in, "w_out": w_out, "grad_update": grad_update}


def normalize(values):
    mean = lax.optimization_barrier(jnp.mean(values, axis=-1, keepdims=True))
    centred = values - mean
    rstd = 1.0 / jnp.sqrt(lax.optimization_barrier(jnp.mean(centred * centred, axis=-1, keepdims=True)) + 1e-05)
    return (centred * rstd, rstd)

def norm_back(grad, normed, rstd):
    return rstd * (grad - lax.optimization_barrier(jnp.mean(grad, axis=-1, keepdims=True)) - normed * lax.optimization_barrier(jnp.mean(grad * normed, axis=-1, keepdims=True)))

def token_valid(positions, chain_tokens, slot):
    chain_of = positions // slot
    offset = positions - chain_of * slot
    onehot = chain_of[:, None] == jnp.arange(chain_tokens.shape[0], dtype=jnp.int32)[None, :]
    count = lax.optimization_barrier(jnp.sum(jnp.where(onehot, chain_tokens[None, :], 0), axis=1))
    return (offset < count).astype(jnp.float32)

def project(values, weight):
    flat = values.reshape(-1, values.shape[-1])
    result = jnp.dot(flat, weight, preferred_element_type=jnp.float32)
    return result.reshape(values.shape[:-1] + (weight.shape[1],))

def reference(pair, chain_tokens, w_in, w_out, grad_update):
    tokens = pair.shape[0]
    width = pair.shape[2]
    slot = tokens // CHAINS
    positions = jnp.arange(tokens, dtype=jnp.int32)
    valid = token_valid(positions, chain_tokens, slot)
    mask = (valid[:, None] * valid[None, :])[:, :, None]
    normed, rstd = normalize(pair.astype(jnp.float32))
    proj = project(normed.astype(jnp.bfloat16), w_in)
    a_lin = proj[..., 0:width]
    a_gate = proj[..., width:2 * width]
    b_lin = proj[..., 2 * width:3 * width]
    b_gate = proj[..., 3 * width:4 * width]
    o_gate = proj[..., 4 * width:5 * width]
    s_a = jax.nn.sigmoid(a_gate)
    s_b = jax.nn.sigmoid(b_gate)
    s_o = jax.nn.sigmoid(o_gate)
    left = (mask * s_a * a_lin).astype(jnp.bfloat16)
    right = (mask * s_b * b_lin).astype(jnp.bfloat16)
    left32 = left.astype(jnp.float32)
    right32 = right.astype(jnp.float32)
    outer = jnp.einsum('kic,kjc->ijc', left32, right32)
    onorm, orstd = normalize(outer)
    value = project(onorm.astype(jnp.bfloat16), w_out)
    update = (s_o * value).astype(jnp.bfloat16)
    grad32 = grad_update.astype(jnp.float32)
    dvb = (grad32 * s_o).astype(jnp.bfloat16)
    du = project(dvb, w_out.T)
    dob = norm_back(du, onorm, orstd).astype(jnp.bfloat16)
    do32 = dob.astype(jnp.float32)
    tj = tokens // N_COL
    ti = tokens // N_ROW

    def left_block(total, index):
        do_part = lax.dynamic_slice_in_dim(do32, (index * tj).astype(jnp.int32), tj, 1)
        right_part = lax.dynamic_slice_in_dim(right32, (index * tj).astype(jnp.int32), tj, 1)
        term = jnp.einsum('ijc,kjc->kic', do_part, right_part)
        return (total + term.astype(jnp.bfloat16).astype(jnp.float32), None)
    dleft, _ = lax.scan(left_block, jnp.zeros((tokens, tokens, width), jnp.float32), jnp.arange(N_COL, dtype=jnp.int32))
    dleft = dleft.astype(jnp.bfloat16).astype(jnp.float32)

    def right_block(total, index):
        do_part = lax.dynamic_slice_in_dim(do32, (index * ti).astype(jnp.int32), ti, 0)
        left_part = lax.dynamic_slice_in_dim(left32, (index * ti).astype(jnp.int32), ti, 1)
        term = jnp.einsum('ijc,kic->kjc', do_part, left_part)
        return (total + term.astype(jnp.bfloat16).astype(jnp.float32), None)
    dright, _ = lax.scan(right_block, jnp.zeros((tokens, tokens, width), jnp.float32), jnp.arange(N_ROW, dtype=jnp.int32))
    d_left = dleft * mask
    d_right = dright * mask
    dproj = jnp.concatenate([d_left * s_a, d_left * a_lin * s_a * (1.0 - s_a), d_right * s_b, d_right * b_lin * s_b * (1.0 - s_b), grad32 * value * s_o * (1.0 - s_o)], axis=2).astype(jnp.bfloat16)
    dx = project(dproj, w_in.T)
    grad_pair = norm_back(dx, normed, rstd).astype(jnp.bfloat16)
    return (update, grad_pair)
```

```python
import functools

import jax
import jax.numpy as jnp
from jax import lax
from jax.experimental import pallas as pl
from jax.experimental.pallas import tpu as pltpu
from jax.sharding import PartitionSpec as P

USE_XLA = False


def normalize(values):
    mean = jnp.mean(values, axis=-1, keepdims=True)
    centred = values - mean
    rstd = 1.0 / jnp.sqrt(jnp.mean(centred * centred, axis=-1, keepdims=True) + 1e-05)
    return (centred * rstd, rstd)


def norm_back(grad, normed, rstd):
    return rstd * (
        grad
        - jnp.mean(grad, axis=-1, keepdims=True)
        - normed * jnp.mean(grad * normed, axis=-1, keepdims=True)
    )


def token_valid(positions, chain_tokens, slot):
    chain_of = positions // slot
    offset = positions - chain_of * slot
    onehot = chain_of[:, None] == jnp.arange(chain_tokens.shape[0], dtype=jnp.int32)[None, :]
    count = jnp.sum(jnp.where(onehot, chain_tokens[None, :], 0), axis=1)
    return (offset < count).astype(jnp.float32)


def exchange_kernel(rows, cols, src, dst, send_sem, recv_sem, own_sem):
    total = rows * cols
    me = lax.axis_index("row") * cols + lax.axis_index("col")
    barrier = pltpu.get_barrier_semaphore()

    def greet(step, carry):
        peer = lax.rem(me + step, total)
        pl.semaphore_signal(
            barrier,
            inc=1,
            device_id=(peer // cols, lax.rem(peer, cols)),
            device_id_type=pl.DeviceIdType.MESH,
        )
        return carry

    own = pltpu.make_async_copy(src.at[me], dst.at[me], own_sem)
    own.start()
    lax.fori_loop(1, total, greet, 0)
    pl.semaphore_wait(barrier, total - 1)

    def copy_to(step):
        peer = lax.rem(me + step, total)
        return pltpu.make_async_remote_copy(
            src_ref=src.at[peer],
            dst_ref=dst.at[me],
            send_sem=send_sem.at[peer],
            recv_sem=recv_sem.at[me],
            device_id=(peer // cols, lax.rem(peer, cols)),
            device_id_type=pl.DeviceIdType.MESH,
        )

    def copy_from(step):
        peer = lax.rem(me + step, total)
        return pltpu.make_async_remote_copy(
            src_ref=src.at[peer],
            dst_ref=dst.at[peer],
            send_sem=send_sem.at[peer],
            recv_sem=recv_sem.at[peer],
            device_id=(peer // cols, lax.rem(peer, cols)),
            device_id_type=pl.DeviceIdType.MESH,
        )

    def send(step, carry):
        copy_to(step).start()
        return carry

    def finish(step, carry):
        copy = copy_from(step)
        copy.wait_send()
        copy.wait_recv()
        return carry

    lax.fori_loop(1, total, send, 0)
    own.wait()
    lax.fori_loop(1, total, finish, 0)


def exchange(blocks, rows, cols, call):
    total = rows * cols
    shape = blocks.shape
    if USE_XLA:
        return lax.all_to_all(blocks, ("row", "col"), split_axis=0, concat_axis=0, tiled=True)
    flat = blocks.reshape(total, -1, 128)
    moved = pl.pallas_call(
        functools.partial(exchange_kernel, rows, cols),
        out_shape=jax.ShapeDtypeStruct(flat.shape, flat.dtype),
        in_specs=[pl.BlockSpec(memory_space=pl.ANY)],
        out_specs=pl.BlockSpec(memory_space=pl.ANY),
        scratch_shapes=[
            pltpu.SemaphoreType.DMA((total,)),
            pltpu.SemaphoreType.DMA((total,)),
            pltpu.SemaphoreType.DMA,
        ],
        compiler_params=pltpu.CompilerParams(collective_id=call, has_side_effects=True),
        name="exchange",
    )(flat)
    return moved.reshape(shape)


def on_device(pair, chain_tokens, w_in, w_out, grad_update):
    rows = lax.axis_size("row")
    cols = lax.axis_size("col")
    tile_i, tile_j, width = pair.shape
    tokens = tile_i * rows
    devices = rows * cols
    own = width // devices
    slot = tokens // chain_tokens.shape[0]

    def to_planes(arrays, call):
        count = len(arrays)
        blocks = jnp.stack([a.reshape(tile_i, tile_j, devices, own) for a in arrays])
        blocks = blocks.transpose(3, 0, 4, 1, 2)
        moved = exchange(blocks, rows, cols, call)
        moved = moved.reshape(rows, cols, count, own, tile_i, tile_j).transpose(2, 3, 0, 4, 1, 5)
        return moved.reshape(count, own, tokens, tokens)

    def to_tiles(planes, call):
        count = len(planes)
        blocks = jnp.stack([p.reshape(own, rows, tile_i, cols, tile_j) for p in planes])
        blocks = blocks.transpose(2, 4, 0, 1, 3, 5).reshape(devices, count, own, tile_i, tile_j)
        moved = exchange(blocks, rows, cols, call)
        return moved.transpose(1, 3, 4, 0, 2).reshape(count, tile_i, tile_j, width)

    row_pos = lax.axis_index("row") * tile_i + jnp.arange(tile_i, dtype=jnp.int32)
    col_pos = lax.axis_index("col") * tile_j + jnp.arange(tile_j, dtype=jnp.int32)
    mask = (
        token_valid(row_pos, chain_tokens, slot)[:, None]
        * token_valid(col_pos, chain_tokens, slot)[None, :]
    )[:, :, None]
    normed, rstd = normalize(pair.astype(jnp.float32))
    proj = jnp.einsum(
        "ijc,cd->ijd", normed.astype(jnp.bfloat16), w_in, preferred_element_type=jnp.float32
    )
    a_lin, a_gate, b_lin, b_gate, o_gate = (
        proj[..., n * width : (n + 1) * width] for n in range(5)
    )
    s_a = jax.nn.sigmoid(a_gate)
    s_b = jax.nn.sigmoid(b_gate)
    s_o = jax.nn.sigmoid(o_gate)
    left = (mask * s_a * a_lin).astype(jnp.bfloat16)
    right = (mask * s_b * b_lin).astype(jnp.bfloat16)
    planes = to_planes([left, right], 0)
    left_p, right_p = planes[0], planes[1]
    outer_p = jnp.einsum("cki,ckj->cij", left_p, right_p, preferred_element_type=jnp.float32)
    outer = to_tiles([outer_p.astype(jnp.bfloat16)], 1)[0].astype(jnp.float32)
    onorm, orstd = normalize(outer)
    value = jnp.einsum(
        "ijc,cd->ijd", onorm.astype(jnp.bfloat16), w_out, preferred_element_type=jnp.float32
    )
    update = (s_o * value).astype(jnp.bfloat16)
    grad32 = grad_update.astype(jnp.float32)
    dvb = (grad32 * s_o).astype(jnp.bfloat16)
    du = jnp.einsum("ijd,cd->ijc", dvb, w_out, preferred_element_type=jnp.float32)
    dob = norm_back(du, onorm, orstd).astype(jnp.bfloat16)
    dob_p = to_planes([dob], 2)[0]
    dleft_p = jnp.einsum("cij,ckj->cki", dob_p, right_p, preferred_element_type=jnp.float32)
    dright_p = jnp.einsum("cij,cki->ckj", dob_p, left_p, preferred_element_type=jnp.float32)
    grads = to_tiles([dleft_p.astype(jnp.bfloat16), dright_p.astype(jnp.bfloat16)], 3)
    d_left = grads[0].astype(jnp.float32) * mask
    d_right = grads[1].astype(jnp.float32) * mask
    dproj = jnp.concatenate(
        [
            d_left * s_a,
            d_left * a_lin * s_a * (1.0 - s_a),
            d_right * s_b,
            d_right * b_lin * s_b * (1.0 - s_b),
            grad32 * value * s_o * (1.0 - s_o),
        ],
        axis=2,
    ).astype(jnp.bfloat16)
    dx = jnp.einsum("ijd,cd->ijc", dproj, w_in, preferred_element_type=jnp.float32)
    grad_pair = norm_back(dx, normed, rstd).astype(jnp.bfloat16)
    return (update, grad_pair)


def solution(mesh):
    return jax.shard_map(
        on_device,
        mesh=mesh,
        in_specs=(P("row", "col", None), P(), P(), P(), P("row", "col", None)),
        out_specs=(P("row", "col", None), P("row", "col", None)),
        check_vma=False,
    )
```

```python
import functools

import jax
import jax.numpy as jnp
from jax import lax
from jax.experimental import pallas as pl
from jax.experimental.pallas import tpu as pltpu
from jax.sharding import PartitionSpec as P

def normalize(values, axis):
    mean = jnp.mean(values, axis=axis, keepdims=True)
    centred = values - mean
    rstd = 1.0 / jnp.sqrt(jnp.mean(centred * centred, axis=axis, keepdims=True) + 1e-05)
    return (centred * rstd, rstd)


def norm_back(grad, normed, rstd, axis):
    return rstd * (
        grad
        - jnp.mean(grad, axis=axis, keepdims=True)
        - normed * jnp.mean(grad * normed, axis=axis, keepdims=True)
    )


def token_valid(positions, chain_tokens, slot):
    chain_of = positions // slot
    offset = positions - chain_of * slot
    onehot = chain_of[:, None] == jnp.arange(chain_tokens.shape[0], dtype=jnp.int32)[None, :]
    count = jnp.sum(jnp.where(onehot, chain_tokens[None, :], 0), axis=1)
    return (offset < count).astype(jnp.float32)


def exchange_kernel(rows, cols, src, dst, send_sem, recv_sem, own_sem):
    total = rows * cols
    me = lax.axis_index("row") * cols + lax.axis_index("col")
    barrier = pltpu.get_barrier_semaphore()

    def greet(step, carry):
        peer = lax.rem(me + step, total)
        pl.semaphore_signal(
            barrier,
            inc=1,
            device_id=(peer // cols, lax.rem(peer, cols)),
            device_id_type=pl.DeviceIdType.MESH,
        )
        return carry

    own = pltpu.make_async_copy(src.at[me], dst.at[me], own_sem)
    own.start()
    lax.fori_loop(1, total, greet, 0)
    pl.semaphore_wait(barrier, total - 1)

    def copy_to(step):
        peer = lax.rem(me + step, total)
        return pltpu.make_async_remote_copy(
            src_ref=src.at[peer],
            dst_ref=dst.at[me],
            send_sem=send_sem.at[peer],
            recv_sem=recv_sem.at[me],
            device_id=(peer // cols, lax.rem(peer, cols)),
            device_id_type=pl.DeviceIdType.MESH,
        )

    def copy_from(step):
        peer = lax.rem(me + step, total)
        return pltpu.make_async_remote_copy(
            src_ref=src.at[peer],
            dst_ref=dst.at[peer],
            send_sem=send_sem.at[peer],
            recv_sem=recv_sem.at[peer],
            device_id=(peer // cols, lax.rem(peer, cols)),
            device_id_type=pl.DeviceIdType.MESH,
        )

    def send(step, carry):
        copy_to(step).start()
        return carry

    def finish(step, carry):
        copy = copy_from(step)
        copy.wait_send()
        copy.wait_recv()
        return carry

    lax.fori_loop(1, total, send, 0)
    own.wait()
    lax.fori_loop(1, total, finish, 0)


def exchange(blocks, rows, cols, call):
    total = rows * cols
    return pl.pallas_call(
        functools.partial(exchange_kernel, rows, cols),
        out_shape=jax.ShapeDtypeStruct(blocks.shape, blocks.dtype),
        in_specs=[pl.BlockSpec(memory_space=pl.ANY)],
        out_specs=pl.BlockSpec(memory_space=pl.ANY),
        scratch_shapes=[
            pltpu.SemaphoreType.DMA((total,)),
            pltpu.SemaphoreType.DMA((total,)),
            pltpu.SemaphoreType.DMA,
        ],
        compiler_params=pltpu.CompilerParams(collective_id=call, has_side_effects=True),
        name="exchange",
    )(blocks)


def gather_plane(blocks, plane, channel, rows, cols, tile_i, tile_j):
    for r in range(rows):
        slab = jnp.concatenate(
            [
                blocks[r * cols + c].astype(jnp.float32)[channel : channel + 1]
                for c in range(cols)
            ],
            axis=0,
        )
        for t in range(tile_j):
            plane[t * cols : (t + 1) * cols, r * tile_i : (r + 1) * tile_i] = slab[
                :, t * tile_i : (t + 1) * tile_i
            ]


def scatter_plane(value, lines, channel, rows, cols, tile_i, tile_j):
    for r in range(rows):
        for t in range(tile_j):
            lines[r, channel, :, t * tile_i : (t + 1) * tile_i] = value[
                t * cols : (t + 1) * cols, r * tile_i : (r + 1) * tile_i
            ]


def write_blocks(lines, out, count, rows, cols):
    for r in range(rows):
        for c in range(cols):
            out[r * cols + c] = jnp.concatenate(
                [lines[r, n][c : c + 1] for n in range(count)], axis=0
            ).astype(jnp.bfloat16)


def natural_rows(tokens, cols, tile_j):
    row = lax.broadcasted_iota(jnp.int32, (tokens, tokens), 0)
    column = lax.broadcasted_iota(jnp.int32, (tokens, tokens), 1)
    wanted = lax.rem(row, tile_j) * cols + row // tile_j
    return jnp.where(column == wanted, 1.0, 0.0).astype(jnp.bfloat16)


def dot(a, b, dims):
    return lax.dot_general(a, b, (dims, ((), ())), preferred_element_type=jnp.float32)


def forward_kernel(sizes, own, blocks, out, planes, plane, lines):
    rows, cols, tile_i, tile_j = sizes
    order = natural_rows(rows * tile_i, cols, tile_j)
    for n in range(own):
        gather_plane(blocks, plane, n, *sizes)
        left = plane[...].astype(jnp.bfloat16)
        planes[n] = left
        gather_plane(blocks, plane, own + n, *sizes)
        right = plane[...].astype(jnp.bfloat16)
        planes[own + n] = right
        left = dot(order, left, ((1,), (0,))).astype(jnp.bfloat16)
        scatter_plane(dot(right, left, ((1,), (1,))), lines, n, *sizes)
    write_blocks(lines, out, own, rows, cols)


def backward_kernel(sizes, own, blocks, planes, out, plane, lines):
    rows, cols, tile_i, tile_j = sizes
    order = natural_rows(rows * tile_i, cols, tile_j)
    for n in range(own):
        gather_plane(blocks, plane, n, *sizes)
        grad = dot(plane[...].astype(jnp.bfloat16), order, ((1,), (0,))).astype(jnp.bfloat16)
        scatter_plane(dot(grad, planes[own + n], ((0,), (0,))), lines, n, *sizes)
        scatter_plane(dot(grad, planes[n], ((1,), (0,))), lines, own + n, *sizes)
    write_blocks(lines, out, 2 * own, rows, cols)


def on_device(pair, chain_tokens, w_in, w_out, grad_update):
    rows = lax.axis_size("row")
    cols = lax.axis_size("col")
    tile_i, tile_j, width = pair.shape
    tokens = tile_i * rows
    devices = rows * cols
    own = width // devices
    entries = tile_i * tile_j
    slot = tokens // chain_tokens.shape[0]
    sizes = (rows, cols, tile_i, tile_j)
    vmem = pl.BlockSpec(memory_space=pltpu.VMEM)

    def scratch(count):
        return [
            pltpu.VMEM((tokens, tokens), jnp.float32),
            pltpu.VMEM((rows, count, cols, entries), jnp.float32),
        ]

    params = pltpu.CompilerParams(vmem_limit_bytes=48 * 1024 * 1024)
    blocks_of = lambda count: jax.ShapeDtypeStruct((devices, count, entries), jnp.bfloat16)

    row_pos = lax.axis_index("row") * tile_i + jnp.arange(tile_i, dtype=jnp.int32)
    col_pos = lax.axis_index("col") * tile_j + jnp.arange(tile_j, dtype=jnp.int32)
    mask = (
        token_valid(col_pos, chain_tokens, slot)[:, None]
        * token_valid(row_pos, chain_tokens, slot)[None, :]
    ).reshape(1, entries)
    x = pair.transpose(1, 0, 2).reshape(entries, width).astype(jnp.float32)
    normed, rstd = normalize(x, 1)
    proj = dot(w_in, normed.astype(jnp.bfloat16), ((0,), (1,)))
    a_lin, a_gate, b_lin, b_gate, o_gate = (
        proj[n * width : (n + 1) * width] for n in range(5)
    )
    s_a = jax.nn.sigmoid(a_gate)
    s_b = jax.nn.sigmoid(b_gate)
    s_o = jax.nn.sigmoid(o_gate)
    left = (mask * s_a * a_lin).astype(jnp.bfloat16).reshape(devices, own, entries)
    right = (mask * s_b * b_lin).astype(jnp.bfloat16).reshape(devices, own, entries)
    moved = exchange(jnp.concatenate([left, right], axis=1), rows, cols, 0)
    outer, planes = pl.pallas_call(
        functools.partial(forward_kernel, sizes, own),
        out_shape=(
            blocks_of(own),
            jax.ShapeDtypeStruct((2 * own, tokens, tokens), jnp.bfloat16),
        ),
        in_specs=[vmem],
        out_specs=(vmem, vmem),
        scratch_shapes=scratch(own),
        compiler_params=params,
        name="outer",
    )(moved)
    outer = exchange(outer, rows, cols, 1).reshape(width, entries).astype(jnp.float32)
    onorm, orstd = normalize(outer, 0)
    value = dot(w_out, onorm.astype(jnp.bfloat16), ((0,), (0,)))
    grad32 = grad_update.transpose(1, 0, 2).reshape(entries, width).T.astype(jnp.float32)
    dvb = (grad32 * s_o).astype(jnp.bfloat16)
    du = dot(w_out, dvb, ((1,), (0,)))
    dob = norm_back(du, onorm, orstd, 0).astype(jnp.bfloat16)
    moved = exchange(dob.reshape(devices, own, entries), rows, cols, 2)
    grads = pl.pallas_call(
        functools.partial(backward_kernel, sizes, own),
        out_shape=blocks_of(2 * own),
        in_specs=[vmem, vmem],
        out_specs=vmem,
        scratch_shapes=scratch(2 * own),
        compiler_params=params,
        name="outer_back",
    )(moved, planes)
    update = (s_o * value).astype(jnp.bfloat16).T
    grads = exchange(grads, rows, cols, 3)
    d_left = grads[:, :own].reshape(width, entries).astype(jnp.float32) * mask
    d_right = grads[:, own:].reshape(width, entries).astype(jnp.float32) * mask
    dproj = jnp.concatenate(
        [
            d_left * s_a,
            d_left * a_lin * s_a * (1.0 - s_a),
            d_right * s_b,
            d_right * b_lin * s_b * (1.0 - s_b),
            grad32 * value * s_o * (1.0 - s_o),
        ],
        axis=0,
    ).astype(jnp.bfloat16)
    dx = dot(dproj, w_in, ((0,), (1,)))
    grad_pair = norm_back(dx, normed, rstd, 1).astype(jnp.bfloat16)

    def home(values):
        return values.reshape(tile_j, tile_i, width).transpose(1, 0, 2)

    return (home(update), home(grad_pair))


def solution(mesh):
    return jax.shard_map(
        on_device,
        mesh=mesh,
        in_specs=(P("row", "col", None), P(), P(), P(), P("row", "col", None)),
        out_specs=(P("row", "col", None), P("row", "col", None)),
        check_vma=False,
    )
```

```python
import functools

import jax
import jax.numpy as jnp
from jax import lax
from jax.experimental import pallas as pl
from jax.experimental.pallas import tpu as pltpu
from jax.sharding import PartitionSpec as P

def normalize(values, axis):
    mean = jnp.mean(values, axis=axis, keepdims=True)
    centred = values - mean
    rstd = 1.0 / jnp.sqrt(jnp.mean(centred * centred, axis=axis, keepdims=True) + 1e-05)
    return (centred * rstd, rstd)


def norm_back(grad, normed, rstd, axis):
    return rstd * (
        grad
        - jnp.mean(grad, axis=axis, keepdims=True)
        - normed * jnp.mean(grad * normed, axis=axis, keepdims=True)
    )


def token_valid(positions, chain_tokens, slot):
    chain_of = positions // slot
    offset = positions - chain_of * slot
    onehot = chain_of[:, None] == jnp.arange(chain_tokens.shape[0], dtype=jnp.int32)[None, :]
    count = jnp.sum(jnp.where(onehot, chain_tokens[None, :], 0), axis=1)
    return (offset < count).astype(jnp.float32)


def greet_all(rows, cols):
    total = rows * cols
    me = lax.axis_index("row") * cols + lax.axis_index("col")
    barrier = pltpu.get_barrier_semaphore()

    def greet(step, carry):
        peer = lax.rem(me + step, total)
        pl.semaphore_signal(
            barrier,
            inc=1,
            device_id=(peer // cols, lax.rem(peer, cols)),
            device_id_type=pl.DeviceIdType.MESH,
        )
        return carry

    lax.fori_loop(1, total, greet, 0)
    pl.semaphore_wait(barrier, total - 1)


def exchange(rows, cols, src, dst, send_sem, recv_sem, own_sem):
    total = rows * cols
    me = lax.axis_index("row") * cols + lax.axis_index("col")

    def copy(step, slot_of):
        peer = lax.rem(me + step, total)
        slot = slot_of(peer)
        return pltpu.make_async_remote_copy(
            src_ref=src.at[peer],
            dst_ref=dst.at[slot],
            send_sem=send_sem.at[peer],
            recv_sem=recv_sem.at[slot],
            device_id=(peer // cols, lax.rem(peer, cols)),
            device_id_type=pl.DeviceIdType.MESH,
        )

    def send(step, carry):
        copy(step, lambda peer: me).start()
        return carry

    def finish(step, carry):
        pending = copy(step, lambda peer: peer)
        pending.wait_send()
        pending.wait_recv()
        return carry

    own = pltpu.make_async_copy(src.at[me], dst.at[me], own_sem)
    lax.fori_loop(1, total, send, 0)
    own.start()
    own.wait()
    lax.fori_loop(1, total, finish, 0)


def gather_plane(blocks, plane, channel, rows, cols, tile_i, tile_j):
    for r in range(rows):
        slab = jnp.concatenate(
            [
                blocks[r * cols + c].astype(jnp.float32)[channel : channel + 1]
                for c in range(cols)
            ],
            axis=0,
        )
        for t in range(tile_j):
            plane[t * cols : (t + 1) * cols, r * tile_i : (r + 1) * tile_i] = slab[
                :, t * tile_i : (t + 1) * tile_i
            ]


def scatter_plane(value, lines, channel, rows, cols, tile_i, tile_j):
    for r in range(rows):
        for t in range(tile_j):
            lines[r, channel, :, t * tile_i : (t + 1) * tile_i] = value[
                t * cols : (t + 1) * cols, r * tile_i : (r + 1) * tile_i
            ]


def write_blocks(lines, out, count, rows, cols):
    for r in range(rows):
        for c in range(cols):
            out[r * cols + c] = jnp.concatenate(
                [lines[r, n][c : c + 1] for n in range(count)], axis=0
            ).astype(jnp.bfloat16)


def natural_rows(tokens, cols, tile_j):
    row = lax.broadcasted_iota(jnp.int32, (tokens, tokens), 0)
    column = lax.broadcasted_iota(jnp.int32, (tokens, tokens), 1)
    wanted = lax.rem(row, tile_j) * cols + row // tile_j
    return jnp.where(column == wanted, 1.0, 0.0).astype(jnp.bfloat16)


def dot(a, b, dims):
    return lax.dot_general(a, b, (dims, ((), ())), preferred_element_type=jnp.float32)


def forward_kernel(sizes, own, blocks, out, planes, plane, lines):
    rows, cols, tile_i, tile_j = sizes
    order = natural_rows(rows * tile_i, cols, tile_j)
    for n in range(own):
        gather_plane(blocks, plane, n, *sizes)
        left = plane[...].astype(jnp.bfloat16)
        planes[n] = left
        gather_plane(blocks, plane, own + n, *sizes)
        right = plane[...].astype(jnp.bfloat16)
        planes[own + n] = right
        left = dot(order, left, ((1,), (0,))).astype(jnp.bfloat16)
        scatter_plane(dot(right, left, ((1,), (1,))), lines, n, *sizes)
    write_blocks(lines, out, own, rows, cols)


def backward_kernel(sizes, own, blocks, planes, out, plane, lines):
    rows, cols, tile_i, tile_j = sizes
    order = natural_rows(rows * tile_i, cols, tile_j)
    for n in range(own):
        gather_plane(blocks, plane, n, *sizes)
        grad = dot(plane[...].astype(jnp.bfloat16), order, ((1,), (0,))).astype(jnp.bfloat16)
        scatter_plane(dot(grad, planes[own + n], ((0,), (0,))), lines, n, *sizes)
        scatter_plane(dot(grad, planes[n], ((1,), (0,))), lines, own + n, *sizes)
    write_blocks(lines, out, 2 * own, rows, cols)


def middle(own, total, received, gate, grad, w_out, update, d_gate, d_outer, chunk):
    width, entries = gate.shape

    def part(index, carry):
        at = pl.ds(pl.multiple_of(index * chunk, chunk), chunk)
        outer = jnp.concatenate(
            [received[d, :, at].astype(jnp.float32) for d in range(total)], axis=0
        )
        s_o = gate[:, at]
        grad32 = grad[:, at].astype(jnp.float32)
        onorm, orstd = normalize(outer, 0)
        value = dot(w_out[...], onorm.astype(jnp.bfloat16), ((0,), (0,)))
        update[:, at] = (s_o * value).astype(jnp.bfloat16)
        d_gate[:, at] = (grad32 * value * s_o * (1.0 - s_o)).astype(jnp.bfloat16)
        du = dot(w_out[...], (grad32 * s_o).astype(jnp.bfloat16), ((1,), (0,)))
        dob = norm_back(du, onorm, orstd, 0).astype(jnp.bfloat16)
        for d in range(total):
            d_outer[d, :, at] = dob[d * own : (d + 1) * own]
        return carry

    lax.fori_loop(0, entries // chunk, part, 0)


def core_kernel(
    sizes,
    own,
    sides,
    gate,
    grad,
    w_out,
    update,
    d_gate,
    grads,
    sides_in,
    outer_out,
    outer_in,
    d_outer,
    d_outer_in,
    grads_out,
    planes,
    plane,
    lines,
    send_sem,
    recv_sem,
    own_sem,
):
    rows, cols, tile_i, tile_j = sizes

    def move(src, dst, phase):
        exchange(
            rows, cols, src, dst, send_sem.at[phase], recv_sem.at[phase], own_sem.at[phase]
        )

    greet_all(rows, cols)
    move(sides, sides_in, 0)
    forward_kernel(sizes, own, sides_in, outer_out, planes, plane, lines)
    move(outer_out, outer_in, 1)
    middle(own, rows * cols, outer_in, gate, grad, w_out, update, d_gate, d_outer, 128)
    move(d_outer, d_outer_in, 2)
    backward_kernel(sizes, own, d_outer_in, planes, grads_out, plane, lines)
    move(grads_out, grads, 3)


def on_device(pair, chain_tokens, w_in, w_out, grad_update):
    rows = lax.axis_size("row")
    cols = lax.axis_size("col")
    tile_i, tile_j, width = pair.shape
    tokens = tile_i * rows
    devices = rows * cols
    own = width // devices
    entries = tile_i * tile_j
    slot = tokens // chain_tokens.shape[0]
    sizes = (rows, cols, tile_i, tile_j)
    vmem = pl.BlockSpec(memory_space=pltpu.VMEM)

    whole = pl.BlockSpec(memory_space=pl.ANY)
    block = lambda count: (devices, count, entries)

    row_pos = lax.axis_index("row") * tile_i + jnp.arange(tile_i, dtype=jnp.int32)
    col_pos = lax.axis_index("col") * tile_j + jnp.arange(tile_j, dtype=jnp.int32)
    mask = (
        token_valid(col_pos, chain_tokens, slot)[:, None]
        * token_valid(row_pos, chain_tokens, slot)[None, :]
    ).reshape(1, entries)
    x = pair.transpose(1, 0, 2).reshape(entries, width).astype(jnp.float32)
    normed, rstd = normalize(x, 1)
    proj = dot(w_in, normed.astype(jnp.bfloat16), ((0,), (1,)))
    a_lin, a_gate, b_lin, b_gate, o_gate = (
        proj[n * width : (n + 1) * width] for n in range(5)
    )
    s_a = jax.nn.sigmoid(a_gate)
    s_b = jax.nn.sigmoid(b_gate)
    s_o = jax.nn.sigmoid(o_gate)
    left = (mask * s_a * a_lin).astype(jnp.bfloat16).reshape(devices, own, entries)
    right = (mask * s_b * b_lin).astype(jnp.bfloat16).reshape(devices, own, entries)
    sides = jnp.concatenate([left, right], axis=1)
    grad_t = grad_update.transpose(1, 0, 2).reshape(entries, width).T
    flat = jax.ShapeDtypeStruct((width, entries), jnp.bfloat16)
    update, d_gate, grads = pl.pallas_call(
        functools.partial(core_kernel, sizes, own),
        out_shape=(flat, flat, jax.ShapeDtypeStruct(block(2 * own), jnp.bfloat16)),
        in_specs=[vmem] * 4,
        out_specs=(vmem, vmem, whole),
        scratch_shapes=[
            pltpu.VMEM(block(2 * own), jnp.bfloat16),
            pltpu.VMEM(block(own), jnp.bfloat16),
            pltpu.VMEM(block(own), jnp.bfloat16),
            pltpu.VMEM(block(own), jnp.bfloat16),
            pltpu.VMEM(block(own), jnp.bfloat16),
            pltpu.VMEM(block(2 * own), jnp.bfloat16),
            pltpu.VMEM((2 * own, tokens, tokens), jnp.bfloat16),
            pltpu.VMEM((tokens, tokens), jnp.float32),
            pltpu.VMEM((rows, 2 * own, cols, entries), jnp.float32),
            pltpu.SemaphoreType.DMA((4, devices)),
            pltpu.SemaphoreType.DMA((4, devices)),
            pltpu.SemaphoreType.DMA((4,)),
        ],
        compiler_params=pltpu.CompilerParams(
            collective_id=0, has_side_effects=True, vmem_limit_bytes=56 * 1024 * 1024
        ),
        name="core",
    )(sides, s_o, grad_t, w_out)
    update = update.T
    d_left = grads[:, :own].reshape(width, entries).astype(jnp.float32) * mask
    d_right = grads[:, own:].reshape(width, entries).astype(jnp.float32) * mask
    dproj = jnp.concatenate(
        [
            d_left * s_a,
            d_left * a_lin * s_a * (1.0 - s_a),
            d_right * s_b,
            d_right * b_lin * s_b * (1.0 - s_b),
        ],
        axis=0,
    ).astype(jnp.bfloat16)
    dproj = jnp.concatenate([dproj, d_gate], axis=0)
    dx = dot(dproj, w_in, ((0,), (1,)))
    grad_pair = norm_back(dx, normed, rstd, 1).astype(jnp.bfloat16)

    def home(values):
        return values.reshape(tile_j, tile_i, width).transpose(1, 0, 2)

    return (home(update), home(grad_pair))


def solution(mesh):
    return jax.shard_map(
        on_device,
        mesh=mesh,
        in_specs=(P("row", "col", None), P(), P(), P(), P("row", "col", None)),
        out_specs=(P("row", "col", None), P("row", "col", None)),
        check_vma=False,
    )
```

```python
import functools

import jax
import jax.numpy as jnp
from jax import lax
from jax.experimental import pallas as pl
from jax.experimental.pallas import tpu as pltpu
from jax.sharding import PartitionSpec as P

def normalize(values, axis):
    mean = jnp.mean(values, axis=axis, keepdims=True)
    centred = values - mean
    rstd = 1.0 / jnp.sqrt(jnp.mean(centred * centred, axis=axis, keepdims=True) + 1e-05)
    return (centred * rstd, rstd)


def norm_back(grad, normed, rstd, axis):
    return rstd * (
        grad
        - jnp.mean(grad, axis=axis, keepdims=True)
        - normed * jnp.mean(grad * normed, axis=axis, keepdims=True)
    )


def token_valid(positions, chain_tokens, slot):
    chain_of = positions // slot
    offset = positions - chain_of * slot
    onehot = chain_of[:, None] == jnp.arange(chain_tokens.shape[0], dtype=jnp.int32)[None, :]
    count = jnp.sum(jnp.where(onehot, chain_tokens[None, :], 0), axis=1)
    return (offset < count).astype(jnp.float32)


def greet_all(rows, cols):
    total = rows * cols
    me = lax.axis_index("row") * cols + lax.axis_index("col")
    barrier = pltpu.get_barrier_semaphore()

    def greet(step, carry):
        peer = lax.rem(me + step, total)
        pl.semaphore_signal(
            barrier,
            inc=1,
            device_id=(peer // cols, lax.rem(peer, cols)),
            device_id_type=pl.DeviceIdType.MESH,
        )
        return carry

    lax.fori_loop(1, total, greet, 0)
    pl.semaphore_wait(barrier, total - 1)


def exchange(rows, cols, src, dst, send_sem, recv_sem, own_sem):
    total = rows * cols
    me = lax.axis_index("row") * cols + lax.axis_index("col")

    def copy(step, slot_of):
        peer = lax.rem(me + step, total)
        slot = slot_of(peer)
        return pltpu.make_async_remote_copy(
            src_ref=src.at[peer],
            dst_ref=dst.at[slot],
            send_sem=send_sem.at[peer],
            recv_sem=recv_sem.at[slot],
            device_id=(peer // cols, lax.rem(peer, cols)),
            device_id_type=pl.DeviceIdType.MESH,
        )

    def send(step, carry):
        copy(step, lambda peer: me).start()
        return carry

    def finish(step, carry):
        pending = copy(step, lambda peer: peer)
        pending.wait_send()
        pending.wait_recv()
        return carry

    own = pltpu.make_async_copy(src.at[me], dst.at[me], own_sem)
    lax.fori_loop(1, total, send, 0)
    own.start()
    own.wait()
    lax.fori_loop(1, total, finish, 0)


def gather_plane(blocks, plane, channel, rows, cols, tile_i, tile_j):
    for r in range(rows):
        slab = jnp.concatenate(
            [
                blocks[r * cols + c].astype(jnp.float32)[channel : channel + 1]
                for c in range(cols)
            ],
            axis=0,
        )
        for t in range(tile_j):
            plane[t * cols : (t + 1) * cols, r * tile_i : (r + 1) * tile_i] = slab[
                :, t * tile_i : (t + 1) * tile_i
            ]


def scatter_plane(value, lines, channel, rows, cols, tile_i, tile_j):
    for r in range(rows):
        for t in range(tile_j):
            lines[r, channel, :, t * tile_i : (t + 1) * tile_i] = value[
                t * cols : (t + 1) * cols, r * tile_i : (r + 1) * tile_i
            ]


def write_blocks(lines, out, count, rows, cols):
    for r in range(rows):
        for c in range(cols):
            out[r * cols + c] = jnp.concatenate(
                [lines[r, n][c : c + 1] for n in range(count)], axis=0
            ).astype(jnp.bfloat16)


def natural_rows(tokens, cols, tile_j):
    row = lax.broadcasted_iota(jnp.int32, (tokens, tokens), 0)
    column = lax.broadcasted_iota(jnp.int32, (tokens, tokens), 1)
    wanted = lax.rem(row, tile_j) * cols + row // tile_j
    return jnp.where(column == wanted, 1.0, 0.0).astype(jnp.bfloat16)


def dot(a, b, dims):
    return lax.dot_general(a, b, (dims, ((), ())), preferred_element_type=jnp.float32)


def forward_kernel(sizes, own, blocks, out, planes, plane, lines):
    rows, cols, tile_i, tile_j = sizes
    order = natural_rows(rows * tile_i, cols, tile_j)
    for n in range(own):
        gather_plane(blocks, plane, n, *sizes)
        left = plane[...].astype(jnp.bfloat16)
        planes[n] = left
        gather_plane(blocks, plane, own + n, *sizes)
        right = plane[...].astype(jnp.bfloat16)
        planes[own + n] = right
        left = dot(order, left, ((1,), (0,))).astype(jnp.bfloat16)
        scatter_plane(dot(right, left, ((1,), (1,))), lines, n, *sizes)
    write_blocks(lines, out, own, rows, cols)


def backward_kernel(sizes, own, blocks, planes, out, plane, lines):
    rows, cols, tile_i, tile_j = sizes
    order = natural_rows(rows * tile_i, cols, tile_j)
    for n in range(own):
        gather_plane(blocks, plane, n, *sizes)
        grad = dot(plane[...].astype(jnp.bfloat16), order, ((1,), (0,))).astype(jnp.bfloat16)
        scatter_plane(dot(grad, planes[own + n], ((0,), (0,))), lines, n, *sizes)
        scatter_plane(dot(grad, planes[n], ((1,), (0,))), lines, own + n, *sizes)
    write_blocks(lines, out, 2 * own, rows, cols)


def first(own, total, x, mask, w_in, proj, sides, chunk):
    entries, width = x.shape

    def part(index, carry):
        at = pl.ds(pl.multiple_of(index * chunk, chunk), chunk)
        normed, _ = normalize(x[at, :].astype(jnp.float32), 1)
        lines = dot(w_in[...], normed.astype(jnp.bfloat16), ((0,), (1,)))
        proj[:, at] = lines
        a_lin, a_gate, b_lin, b_gate = (lines[n * width : (n + 1) * width] for n in range(4))
        left = mask[:, at] * jax.nn.sigmoid(a_gate) * a_lin
        right = mask[:, at] * jax.nn.sigmoid(b_gate) * b_lin
        for d in range(total):
            own_rows = slice(d * own, (d + 1) * own)
            sides[d, :, at] = jnp.concatenate([left[own_rows], right[own_rows]], axis=0).astype(
                jnp.bfloat16
            )
        return carry

    lax.fori_loop(0, entries // chunk, part, 0)


def middle(own, total, received, proj, grad, w_out, update, d_gate, d_outer, chunk):
    entries, width = grad.shape

    def part(index, carry):
        at = pl.ds(pl.multiple_of(index * chunk, chunk), chunk)
        outer = jnp.concatenate(
            [received[d, :, at].astype(jnp.float32) for d in range(total)], axis=0
        )
        s_o = jax.nn.sigmoid(proj[4 * width : 5 * width, at])
        grad32 = grad[at, :].astype(jnp.float32).T
        onorm, orstd = normalize(outer, 0)
        value = dot(w_out[...], onorm.astype(jnp.bfloat16), ((0,), (0,)))
        update[at, :] = (s_o * value).T.astype(jnp.bfloat16)
        d_gate[:, at] = (grad32 * value * s_o * (1.0 - s_o)).astype(jnp.bfloat16)
        du = dot(w_out[...], (grad32 * s_o).astype(jnp.bfloat16), ((1,), (0,)))
        dob = norm_back(du, onorm, orstd, 0).astype(jnp.bfloat16)
        for d in range(total):
            d_outer[d, :, at] = dob[d * own : (d + 1) * own]
        return carry

    lax.fori_loop(0, entries // chunk, part, 0)


def last(own, total, x, mask, w_in, proj, grads, d_gate, grad_pair, chunk):
    entries, width = x.shape

    def part(index, carry):
        at = pl.ds(pl.multiple_of(index * chunk, chunk), chunk)
        arrived = [grads[d, :, at].astype(jnp.float32) for d in range(total)]
        d_left = jnp.concatenate([block[:own] for block in arrived], axis=0) * mask[:, at]
        d_right = jnp.concatenate([block[own:] for block in arrived], axis=0) * mask[:, at]
        a_lin, a_gate, b_lin, b_gate = (
            proj[n * width : (n + 1) * width, at] for n in range(4)
        )
        s_a = jax.nn.sigmoid(a_gate)
        s_b = jax.nn.sigmoid(b_gate)
        parts = [
            d_left * s_a,
            d_left * a_lin * s_a * (1.0 - s_a),
            d_right * s_b,
            d_right * b_lin * s_b * (1.0 - s_b),
        ]
        dproj = jnp.concatenate([p.astype(jnp.bfloat16) for p in parts] + [d_gate[:, at]], axis=0)
        dx = dot(dproj, w_in[...], ((0,), (1,)))
        normed, rstd = normalize(x[at, :].astype(jnp.float32), 1)
        grad_pair[at, :] = norm_back(dx, normed, rstd, 1).astype(jnp.bfloat16)
        return carry

    lax.fori_loop(0, entries // chunk, part, 0)


def core_kernel(
    sizes,
    own,
    x,
    mask,
    w_in,
    w_out,
    grad,
    update,
    grad_pair,
    proj,
    d_gate,
    sides,
    sides_in,
    outer_out,
    outer_in,
    d_outer,
    d_outer_in,
    grads_out,
    grads,
    planes,
    plane,
    lines,
    send_sem,
    recv_sem,
    own_sem,
):
    rows, cols, tile_i, tile_j = sizes
    total = rows * cols

    def move(src, dst, phase):
        exchange(
            rows, cols, src, dst, send_sem.at[phase], recv_sem.at[phase], own_sem.at[phase]
        )

    first(own, total, x, mask, w_in, proj, sides, 128)
    greet_all(rows, cols)
    move(sides, sides_in, 0)
    forward_kernel(sizes, own, sides_in, outer_out, planes, plane, lines)
    move(outer_out, outer_in, 1)
    middle(own, total, outer_in, proj, grad, w_out, update, d_gate, d_outer, 128)
    move(d_outer, d_outer_in, 2)
    backward_kernel(sizes, own, d_outer_in, planes, grads_out, plane, lines)
    move(grads_out, grads, 3)
    last(own, total, x, mask, w_in, proj, grads, d_gate, grad_pair, 128)


def on_device(pair, chain_tokens, w_in, w_out, grad_update):
    rows = lax.axis_size("row")
    cols = lax.axis_size("col")
    tile_i, tile_j, width = pair.shape
    tokens = tile_i * rows
    devices = rows * cols
    own = width // devices
    entries = tile_i * tile_j
    slot = tokens // chain_tokens.shape[0]
    sizes = (rows, cols, tile_i, tile_j)
    vmem = pl.BlockSpec(memory_space=pltpu.VMEM)
    block = lambda count: pltpu.VMEM((devices, count, entries), jnp.bfloat16)

    row_pos = lax.axis_index("row") * tile_i + jnp.arange(tile_i, dtype=jnp.int32)
    col_pos = lax.axis_index("col") * tile_j + jnp.arange(tile_j, dtype=jnp.int32)
    mask = (
        token_valid(col_pos, chain_tokens, slot)[:, None]
        * token_valid(row_pos, chain_tokens, slot)[None, :]
    ).reshape(1, entries)

    def turned(values):
        return values.transpose(1, 0, 2).reshape(entries, width)

    def home(values):
        return values.reshape(tile_j, tile_i, width).transpose(1, 0, 2)

    flat = jax.ShapeDtypeStruct((entries, width), jnp.bfloat16)
    update, grad_pair = pl.pallas_call(
        functools.partial(core_kernel, sizes, own),
        out_shape=(flat, flat),
        in_specs=[vmem] * 5,
        out_specs=(vmem, vmem),
        scratch_shapes=[
            pltpu.VMEM((5 * width, entries), jnp.float32),
            pltpu.VMEM((width, entries), jnp.bfloat16),
            block(2 * own),
            block(2 * own),
            block(own),
            block(own),
            block(own),
            block(own),
            block(2 * own),
            block(2 * own),
            pltpu.VMEM((2 * own, tokens, tokens), jnp.bfloat16),
            pltpu.VMEM((tokens, tokens), jnp.float32),
            pltpu.VMEM((rows, 2 * own, cols, entries), jnp.float32),
            pltpu.SemaphoreType.DMA((4, devices)),
            pltpu.SemaphoreType.DMA((4, devices)),
            pltpu.SemaphoreType.DMA((4,)),
        ],
        compiler_params=pltpu.CompilerParams(
            collective_id=0, has_side_effects=True, vmem_limit_bytes=56 * 1024 * 1024
        ),
        name="core",
    )(turned(pair), mask, w_in, w_out, turned(grad_update))
    return (home(update), home(grad_pair))


def solution(mesh):
    return jax.shard_map(
        on_device,
        mesh=mesh,
        in_specs=(P("row", "col", None), P(), P(), P(), P("row", "col", None)),
        out_specs=(P("row", "col", None), P("row", "col", None)),
        check_vma=False,
    )
```

```python
import functools

import jax
import jax.numpy as jnp
from jax import lax
from jax.experimental import pallas as pl
from jax.experimental.pallas import tpu as pltpu
from jax.sharding import PartitionSpec as P

def normalize(values, axis):
    mean = jnp.mean(values, axis=axis, keepdims=True)
    centred = values - mean
    rstd = 1.0 / jnp.sqrt(jnp.mean(centred * centred, axis=axis, keepdims=True) + 1e-05)
    return (centred * rstd, rstd)


def norm_back(grad, normed, rstd, axis):
    return rstd * (
        grad
        - jnp.mean(grad, axis=axis, keepdims=True)
        - normed * jnp.mean(grad * normed, axis=axis, keepdims=True)
    )


def token_valid(positions, chain_tokens, slot):
    chain_of = positions // slot
    offset = positions - chain_of * slot
    onehot = chain_of[:, None] == jnp.arange(chain_tokens.shape[0], dtype=jnp.int32)[None, :]
    count = jnp.sum(jnp.where(onehot, chain_tokens[None, :], 0), axis=1)
    return (offset < count).astype(jnp.float32)


def greet_all(rows, cols):
    total = rows * cols
    me = lax.axis_index("row") * cols + lax.axis_index("col")
    barrier = pltpu.get_barrier_semaphore()

    def greet(step, carry):
        peer = lax.rem(me + step, total)
        pl.semaphore_signal(
            barrier,
            inc=1,
            device_id=(peer // cols, lax.rem(peer, cols)),
            device_id_type=pl.DeviceIdType.MESH,
        )
        return carry

    lax.fori_loop(1, total, greet, 0)


def exchange(rows, cols, src, dst, send_sem, recv_sem, own_sem):
    total = rows * cols
    me = lax.axis_index("row") * cols + lax.axis_index("col")

    def copy(step, slot_of):
        peer = lax.rem(me + step, total)
        slot = slot_of(peer)
        return pltpu.make_async_remote_copy(
            src_ref=src.at[peer],
            dst_ref=dst.at[slot],
            send_sem=send_sem.at[peer],
            recv_sem=recv_sem.at[slot],
            device_id=(peer // cols, lax.rem(peer, cols)),
            device_id_type=pl.DeviceIdType.MESH,
        )

    def send(step, carry):
        copy(step, lambda peer: me).start()
        return carry

    def finish(step, carry):
        pending = copy(step, lambda peer: peer)
        pending.wait_send()
        pending.wait_recv()
        return carry

    own = pltpu.make_async_copy(src.at[me], dst.at[me], own_sem)
    lax.fori_loop(1, total, send, 0)
    own.start()
    own.wait()
    lax.fori_loop(1, total, finish, 0)


def gather_plane(blocks, plane, channel, rows, cols, tile_i, tile_j):
    for r in range(rows):
        slab = jnp.concatenate(
            [
                blocks[r * cols + c].astype(jnp.float32)[channel : channel + 1]
                for c in range(cols)
            ],
            axis=0,
        )
        for t in range(tile_j):
            plane[t * cols : (t + 1) * cols, r * tile_i : (r + 1) * tile_i] = slab[
                :, t * tile_i : (t + 1) * tile_i
            ]


def scatter_plane(value, lines, channel, rows, cols, tile_i, tile_j):
    for r in range(rows):
        for t in range(tile_j):
            lines[r, channel, :, t * tile_i : (t + 1) * tile_i] = value[
                t * cols : (t + 1) * cols, r * tile_i : (r + 1) * tile_i
            ]


def write_blocks(lines, out, count, rows, cols):
    for r in range(rows):
        for c in range(cols):
            out[r * cols + c] = jnp.concatenate(
                [lines[r, n][c : c + 1] for n in range(count)], axis=0
            ).astype(jnp.bfloat16)


def natural_rows(tokens, cols, tile_j):
    row = lax.broadcasted_iota(jnp.int32, (tokens, tokens), 0)
    column = lax.broadcasted_iota(jnp.int32, (tokens, tokens), 1)
    wanted = lax.rem(row, tile_j) * cols + row // tile_j
    return jnp.where(column == wanted, 1.0, 0.0).astype(jnp.bfloat16)


def dot(a, b, dims):
    return lax.dot_general(a, b, (dims, ((), ())), preferred_element_type=jnp.float32)


def forward_kernel(sizes, own, blocks, out, planes, plane, lines):
    rows, cols, tile_i, tile_j = sizes
    order = natural_rows(rows * tile_i, cols, tile_j)
    for n in range(own):
        gather_plane(blocks, plane, n, *sizes)
        left = plane[...].astype(jnp.bfloat16)
        planes[n] = left
        gather_plane(blocks, plane, own + n, *sizes)
        right = plane[...].astype(jnp.bfloat16)
        planes[own + n] = right
        left = dot(order, left, ((1,), (0,))).astype(jnp.bfloat16)
        scatter_plane(dot(right, left, ((1,), (1,))), lines, n, *sizes)
    write_blocks(lines, out, own, rows, cols)


def backward_kernel(sizes, own, blocks, planes, out, plane, lines):
    rows, cols, tile_i, tile_j = sizes
    order = natural_rows(rows * tile_i, cols, tile_j)
    for n in range(own):
        gather_plane(blocks, plane, n, *sizes)
        grad = dot(plane[...].astype(jnp.bfloat16), order, ((1,), (0,))).astype(jnp.bfloat16)
        scatter_plane(dot(grad, planes[own + n], ((0,), (0,))), lines, n, *sizes)
        scatter_plane(dot(grad, planes[n], ((1,), (0,))), lines, own + n, *sizes)
    write_blocks(lines, out, 2 * own, rows, cols)


def first(own, total, x, mask, w_in, proj, sides, chunk):
    entries, width = x.shape

    def part(index, carry):
        at = pl.ds(pl.multiple_of(index * chunk, chunk), chunk)
        normed, _ = normalize(x[at, :].astype(jnp.float32), 1)
        lines = dot(w_in[...], normed.astype(jnp.bfloat16), ((0,), (1,)))
        proj[:, at] = lines
        a_lin, a_gate, b_lin, b_gate = (lines[n * width : (n + 1) * width] for n in range(4))
        left = mask[:, at] * jax.nn.sigmoid(a_gate) * a_lin
        right = mask[:, at] * jax.nn.sigmoid(b_gate) * b_lin
        for d in range(total):
            own_rows = slice(d * own, (d + 1) * own)
            sides[d, :, at] = jnp.concatenate([left[own_rows], right[own_rows]], axis=0).astype(
                jnp.bfloat16
            )
        return carry

    lax.fori_loop(0, entries // chunk, part, 0)


def middle(own, total, received, proj, grad, w_out, update, d_gate, d_outer, chunk):
    entries, width = grad.shape

    def part(index, carry):
        at = pl.ds(pl.multiple_of(index * chunk, chunk), chunk)
        outer = jnp.concatenate(
            [received[d, :, at].astype(jnp.float32) for d in range(total)], axis=0
        )
        s_o = jax.nn.sigmoid(proj[4 * width : 5 * width, at])
        grad32 = grad[at, :].astype(jnp.float32).T
        onorm, orstd = normalize(outer, 0)
        value = dot(w_out[...], onorm.astype(jnp.bfloat16), ((0,), (0,)))
        update[at, :] = (s_o * value).T.astype(jnp.bfloat16)
        d_gate[:, at] = (grad32 * value * s_o * (1.0 - s_o)).astype(jnp.bfloat16)
        du = dot(w_out[...], (grad32 * s_o).astype(jnp.bfloat16), ((1,), (0,)))
        dob = norm_back(du, onorm, orstd, 0).astype(jnp.bfloat16)
        for d in range(total):
            d_outer[d, :, at] = dob[d * own : (d + 1) * own]
        return carry

    lax.fori_loop(0, entries // chunk, part, 0)


def last(own, total, x, mask, w_in, proj, grads, d_gate, grad_pair, chunk):
    entries, width = x.shape

    def part(index, carry):
        at = pl.ds(pl.multiple_of(index * chunk, chunk), chunk)
        arrived = [grads[d, :, at].astype(jnp.float32) for d in range(total)]
        d_left = jnp.concatenate([block[:own] for block in arrived], axis=0) * mask[:, at]
        d_right = jnp.concatenate([block[own:] for block in arrived], axis=0) * mask[:, at]
        a_lin, a_gate, b_lin, b_gate = (
            proj[n * width : (n + 1) * width, at] for n in range(4)
        )
        s_a = jax.nn.sigmoid(a_gate)
        s_b = jax.nn.sigmoid(b_gate)
        parts = [
            d_left * s_a,
            d_left * a_lin * s_a * (1.0 - s_a),
            d_right * s_b,
            d_right * b_lin * s_b * (1.0 - s_b),
        ]
        dproj = jnp.concatenate([p.astype(jnp.bfloat16) for p in parts] + [d_gate[:, at]], axis=0)
        dx = dot(dproj, w_in[...], ((0,), (1,)))
        normed, rstd = normalize(x[at, :].astype(jnp.float32), 1)
        grad_pair[at, :] = norm_back(dx, normed, rstd, 1).astype(jnp.bfloat16)
        return carry

    lax.fori_loop(0, entries // chunk, part, 0)


def core_kernel(
    sizes,
    own,
    x,
    mask,
    w_in,
    w_out,
    grad,
    update,
    grad_pair,
    proj,
    d_gate,
    sides,
    sides_in,
    outer_out,
    outer_in,
    d_outer,
    d_outer_in,
    grads_out,
    grads,
    planes,
    plane,
    lines,
    send_sem,
    recv_sem,
    own_sem,
):
    rows, cols, tile_i, tile_j = sizes
    total = rows * cols

    def move(src, dst, phase):
        exchange(
            rows, cols, src, dst, send_sem.at[phase], recv_sem.at[phase], own_sem.at[phase]
        )

    greet_all(rows, cols)
    first(own, total, x, mask, w_in, proj, sides, 128)
    pl.semaphore_wait(pltpu.get_barrier_semaphore(), total - 1)
    move(sides, sides_in, 0)
    forward_kernel(sizes, own, sides_in, outer_out, planes, plane, lines)
    move(outer_out, outer_in, 1)
    middle(own, total, outer_in, proj, grad, w_out, update, d_gate, d_outer, 128)
    move(d_outer, d_outer_in, 2)
    backward_kernel(sizes, own, d_outer_in, planes, grads_out, plane, lines)
    move(grads_out, grads, 3)
    last(own, total, x, mask, w_in, proj, grads, d_gate, grad_pair, 128)


def on_device(pair, chain_tokens, w_in, w_out, grad_update):
    rows = lax.axis_size("row")
    cols = lax.axis_size("col")
    tile_i, tile_j, width = pair.shape
    tokens = tile_i * rows
    devices = rows * cols
    own = width // devices
    entries = tile_i * tile_j
    slot = tokens // chain_tokens.shape[0]
    sizes = (rows, cols, tile_i, tile_j)
    vmem = pl.BlockSpec(memory_space=pltpu.VMEM)
    block = lambda count: pltpu.VMEM((devices, count, entries), jnp.bfloat16)

    row_pos = lax.axis_index("row") * tile_i + jnp.arange(tile_i, dtype=jnp.int32)
    col_pos = lax.axis_index("col") * tile_j + jnp.arange(tile_j, dtype=jnp.int32)
    mask = (
        token_valid(col_pos, chain_tokens, slot)[:, None]
        * token_valid(row_pos, chain_tokens, slot)[None, :]
    ).reshape(1, entries)

    def turned(values):
        return values.transpose(1, 0, 2).reshape(entries, width)

    def home(values):
        return values.reshape(tile_j, tile_i, width).transpose(1, 0, 2)

    flat = jax.ShapeDtypeStruct((entries, width), jnp.bfloat16)
    update, grad_pair = pl.pallas_call(
        functools.partial(core_kernel, sizes, own),
        out_shape=(flat, flat),
        in_specs=[vmem] * 5,
        out_specs=(vmem, vmem),
        scratch_shapes=[
            pltpu.VMEM((5 * width, entries), jnp.float32),
            pltpu.VMEM((width, entries), jnp.bfloat16),
            block(2 * own),
            block(2 * own),
            block(own),
            block(own),
            block(own),
            block(own),
            block(2 * own),
            block(2 * own),
            pltpu.VMEM((2 * own, tokens, tokens), jnp.bfloat16),
            pltpu.VMEM((tokens, tokens), jnp.float32),
            pltpu.VMEM((rows, 2 * own, cols, entries), jnp.float32),
            pltpu.SemaphoreType.DMA((4, devices)),
            pltpu.SemaphoreType.DMA((4, devices)),
            pltpu.SemaphoreType.DMA((4,)),
        ],
        compiler_params=pltpu.CompilerParams(
            collective_id=0, has_side_effects=True, vmem_limit_bytes=56 * 1024 * 1024
        ),
        name="core",
    )(turned(pair), mask, w_in, w_out, turned(grad_update))
    return (home(update), home(grad_pair))


def solution(mesh):
    return jax.shard_map(
        on_device,
        mesh=mesh,
        in_specs=(P("row", "col", None), P(), P(), P(), P("row", "col", None)),
        out_specs=(P("row", "col", None), P("row", "col", None)),
        check_vma=False,
    )
```
